512 devices in a mesh: prow: 64 (over x, z), pcol: 8 (over y, core).
Axes of the slice: x: 4, y: 4, z: 16, core: 2. Of those that a mesh axis runs over, the one named last changes fastest.
Arguments:
- matrix: float32 [16384, 4096], P('prow', 'pcol'), may hold values from -6 to 6
- pivots: int32 [512], replicated, may hold values from 512 to 16383, as said below
- lower_inv: float32 [4, 128, 128], replicated, as said below
- upper_inv: float32 [4, 128, 128], replicated, as said below
Outputs:
- factored: float32 [16384, 4096], P('prow', 'pcol')
The draws below stay inside these ranges and needn't reach their ends.
Inputs may be any that keep to these rules, and one draw needn't show every extreme that they name: The pivots are distinct and each names a row below the first 512 rows; both ends of the range occur in every draw. `lower_inv`: each block is lower triangular with a positive diagonal. `upper_inv`: each block is upper triangular with a positive diagonal.
All inputs are finite; a program needn't handle non-finite values.
Results may differ from the reference program's by a relative error of at most 0.00014.
Values sent between devices are 32-bit elements; how exact they have to be, the bound alone decides.
No kernel may reach another device: no remote copies, remote signals or barrier semaphores. Data moves between devices by JAX's collectives and lax.ppermute only.
A program may use at most 64 MiB of HBM per device.

```python
import math
import jax
import jax.numpy as jnp
from jax import lax

NB = 512
IB = 128
N = 16384
NCOLS = 4096


def draw_pivots(key, part):
    key = jax.random.fold_in(key, 11)
    first_key, second_key = jax.random.split(key)
    middle = jax.random.permutation(first_key, N - NB - 2)[:NB - 2].astype(jnp.int32) + NB + 1
    values = jnp.concatenate([jnp.array([NB, N - 1], dtype=jnp.int32), middle])
    order = jax.random.permutation(second_key, NB)
    return values[order].astype(jnp.int32)


def triangle_noise(noise_key, spread):
    return jax.random.normal(noise_key, (NB // IB, IB, IB), jnp.float32) * spread


def draw_lower_inv(key, part):
    key = jax.random.fold_in(key, 23)
    noise_key, diag_key = jax.random.split(key)
    noise = triangle_noise(noise_key, 0.5 / math.sqrt(IB))
    diagonal = jnp.exp(jax.random.uniform(diag_key, (NB // IB, IB), jnp.float32, -0.5, 0.5))
    index = jnp.arange(IB)
    below = index[:, None] > index[None, :]
    eye_block = jnp.eye(IB, dtype=jnp.float32)
    return jnp.where(below[None], noise, jnp.float32(0.0)) + diagonal[:, :, None] * eye_block[None]


def draw_upper_inv(key, part):
    key = jax.random.fold_in(key, 37)
    noise_key, diag_key = jax.random.split(key)
    noise = triangle_noise(noise_key, 0.5 / math.sqrt(IB))
    diagonal = jnp.exp(jax.random.uniform(diag_key, (NB // IB, IB), jnp.float32, -0.5, 0.5))
    index = jnp.arange(IB)
    above = index[:, None] < index[None, :]
    eye_block = jnp.eye(IB, dtype=jnp.float32)
    whole = jnp.where(above[None], noise, jnp.float32(0.0)) + diagonal[:, :, None] * eye_block[None]
    return whole * (0.5 / math.sqrt(IB))


def shard_levels(key, dims, cuts, low, high):
    level, own = 1.0, jax.random.fold_in(key, 6)
    for axis_at, shards_of in cuts:
        heights = jnp.exp(jax.random.uniform(jax.random.fold_in(own, axis_at), (shards_of,), jnp.float32, low / len(cuts), high / len(cuts)))
        level = level * jnp.repeat(heights, dims[axis_at] // shards_of).reshape([-1 if axis == axis_at else 1 for axis in range(len(dims))])
    return level


def centred(rng, dims, deviation, reach, pieces=(), held_as=jnp.bfloat16):
    result = deviation * jax.random.normal(rng, dims, jnp.float32)
    if pieces:
        result = result * shard_levels(rng, dims, pieces, -0.22, 0.18)
    return jnp.clip(result, -reach, reach).astype(held_as)


def setup_inputs(seed: int = 0) -> dict:
    seeds = jax.random.split(jax.random.key(seed), 5)
    matrix = centred(seeds[0], (N, NCOLS), 1.0, 6.0, ((0, 64), (1, 8)), jnp.float32)
    pivots = draw_pivots(jax.random.fold_in(seeds[4], 71), 0)
    lower_inv = draw_lower_inv(jax.random.fold_in(seeds[4], 71), 0)
    upper_inv = draw_upper_inv(jax.random.fold_in(seeds[4], 71), 0)
    return {"matrix": matrix, "pivots": pivots, "lower_inv": lower_inv, "upper_inv": upper_inv}


def product(left, right):
    return jnp.dot(left, right, precision=lax.Precision.HIGHEST, preferred_element_type=jnp.float32)


def reference(matrix, pivots, lower_inv, upper_inv):
    top_rows = jnp.arange(NB, dtype=jnp.int32)
    swapped = matrix.at[pivots].set(matrix[:NB])
    swapped = swapped.at[top_rows].set(matrix[pivots])
    panel = swapped[:, :NB]
    columns = jnp.arange(NB, dtype=jnp.int32)
    upper_blocks = []
    lower_blocks = []
    for block in range(NB // IB):
        begin_col = block * IB
        end_col = begin_col + IB
        upper_block = product(lower_inv[block], panel[begin_col:end_col])
        lower_block = product(panel[:, begin_col:end_col], upper_inv[block])
        panel = panel.at[:, end_col:].add(-product(lower_block, upper_block[:, end_col:]))
        upper_blocks.append(jnp.where(columns[None, :] >= begin_col, upper_block, jnp.float32(0.0)))
        lower_blocks.append(lower_block)
    lower_all = jnp.concatenate(lower_blocks, axis=1)
    trailing = swapped[:, NB:]
    remainder = trailing[:NB]
    urow_blocks = []
    for block in range(NB // IB):
        begin_col = block * IB
        end_col = begin_col + IB
        urow_block = product(lower_inv[block], remainder[begin_col:end_col])
        remainder = remainder.at[end_col:].add(-product(lower_all[end_col:NB, begin_col:end_col], urow_block))
        trailing = trailing - product(lower_all[:, begin_col:end_col], urow_block)
        urow_blocks.append(urow_block)
    top_part = jnp.concatenate([jnp.concatenate(upper_blocks, axis=0), jnp.concatenate(urow_blocks, axis=0)], axis=1)
    rest_part = jnp.concatenate([lower_all[NB:], trailing[NB:]], axis=1)
    return jnp.concatenate([top_part, rest_part], axis=0)
```

```python
import functools

import jax
import jax.numpy as jnp
from jax import lax
from jax.experimental import pallas as pl
from jax.experimental.pallas import tpu as pltpu
from jax.sharding import PartitionSpec as P

ROWS = 256
NB = 512
IB = 128
BLOCKS = NB // IB
XN = 4
ZN = 16
CAP_OWN = 24
CAP_X = 176
CAP_ZB = 96
CAP_Z = 40

VMEM = pl.BlockSpec(memory_space=pltpu.VMEM)
SMEM = pl.BlockSpec(memory_space=pltpu.SMEM)
PARAMS = pltpu.CompilerParams(vmem_limit_bytes=48 * 1024 * 1024)
F32 = jnp.float32
BF16 = jnp.bfloat16


def product(left, right):
    return jnp.dot(left, right, precision=lax.Precision.HIGHEST, preferred_element_type=F32)


def exact_parts(values):
    high = values.astype(BF16)
    rest = values - high.astype(F32)
    middle = rest.astype(BF16)
    low = (rest - middle.astype(F32)).astype(BF16)
    return high, middle, low


def pick(chosen, values):
    high, middle, low = exact_parts(values)
    small = jnp.dot(chosen, middle, preferred_element_type=F32) + jnp.dot(
        chosen, low, preferred_element_type=F32
    )
    return jnp.dot(chosen, high, preferred_element_type=F32) + small


def ones_at(condition):
    return jnp.where(condition, F32(1.0), F32(0.0)).astype(BF16)


def match(slots, key, mask=None):
    rows = lax.broadcasted_iota(jnp.int32, (slots, key.shape[1]), 0)
    if mask is not None:
        key = jnp.where(mask, key, -1)
    return ones_at(rows == key)


def joined(target, source):
    both = lax.dot_general(target, source, (((1,), (1,)), ((), ())), preferred_element_type=F32)
    return both.astype(BF16)


def unpack(pivots):
    owner = pivots >> 8
    index = lax.broadcasted_iota(jnp.int32, pivots.shape, 1)
    return owner, pivots & 255, owner >> 4, owner & 15, index >> 8


def prep_kernel(place, piv_ref, mat_ref, ranks_ref, cols_ref, asend_ref, dmsg_ref, ok_ref):
    row = place[0]
    pivots = piv_ref[...]
    owner, local, x_of, z_of, half = unpack(pivots)
    classes = jnp.concatenate(
        [
            match(64, owner),
            match(16, x_of),
            match(16, half * 4 + (z_of >> 2)),
            match(32, half * 16 + z_of),
        ],
        axis=0,
    )
    before = ones_at(
        lax.broadcasted_iota(jnp.int32, (NB, NB), 0) < lax.broadcasted_iota(jnp.int32, (NB, NB), 1)
    )
    counts = jnp.dot(classes, before, preferred_element_type=F32) * classes.astype(F32)
    own = jnp.sum(counts[:64], axis=0, keepdims=True)
    in_x = jnp.sum(counts[64:80], axis=0, keepdims=True)
    in_zb = jnp.sum(counts[80:96], axis=0, keepdims=True)
    in_z = jnp.sum(counts[96:128], axis=0, keepdims=True)
    fits = (
        (jnp.max(own) < CAP_OWN)
        & (jnp.max(in_x) < CAP_X)
        & (jnp.max(in_zb) < CAP_ZB)
        & (jnp.max(in_z) < CAP_Z)
    )
    ok_ref[0] = jnp.where(fits, 1, 0).astype(jnp.int32)
    zero = jnp.zeros_like(own)
    ranks = jnp.concatenate([own, in_x, in_zb, in_z, zero, zero, zero, zero], axis=0)
    ranks_ref[...] = ranks.astype(jnp.int32)
    wanted = jnp.concatenate(
        [x_of.astype(F32), jnp.minimum(in_x, 255.0), zero, zero, zero, zero, zero, zero], axis=0
    ).astype(BF16)
    diagonal = ones_at(
        lax.broadcasted_iota(jnp.int32, (NB, NB), 0) == lax.broadcasted_iota(jnp.int32, (NB, NB), 1)
    )
    cols_ref[...] = lax.dot_general(
        diagonal, wanted, (((1,), (1,)), ((), ())), preferred_element_type=F32
    ).astype(jnp.int32)
    own_rank = own.astype(jnp.int32)
    chosen = joined(match(CAP_OWN, own_rank, owner == row), match(ROWS, local))
    asend_ref[...] = pick(chosen, mat_ref[...])

    @pl.when(row < 2)
    def _():
        rank = in_zb.astype(jnp.int32)
        block = z_of >> 2
        rank = jnp.where(row == 0, rank[:, :ROWS], rank[:, ROWS:])
        block = jnp.where(row == 0, block[:, :ROWS], block[:, ROWS:])
        chosen = jnp.concatenate([match(CAP_ZB, rank, block == a) for a in range(4)], axis=0)
        dmsg_ref[...] = pick(chosen, mat_ref[...])


def group_kernel(place, piv_ref, ranks_ref, gathered_ref, amsg_ref):
    row = place[0]
    owner, local, x_of, z_of, half = unpack(piv_ref[...])
    ranks = ranks_ref[...]
    target = match(CAP_X, ranks[1:2], x_of == (row >> 4))
    source = match(ZN * CAP_OWN, z_of * CAP_OWN + ranks[0:1])
    amsg_ref[...] = pick(joined(target, source), gathered_ref[...])


def near_kernel(place, piv_ref, ranks_ref, dmsg_ref, r1_ref, r2_ref, r3_ref, m0, m1, m2, m3):
    row = place[0]

    @pl.when((row < ZN) & ((row & 3) < 2))
    def _():
        owner, local, x_of, z_of, half = unpack(piv_ref[...])
        ranks = ranks_ref[...]
        side = row & 1
        rows = jnp.where(row < 2, dmsg_ref[:CAP_ZB], r1_ref[...] + r2_ref[...] + r3_ref[...])
        source = match(CAP_ZB, ranks[2:3])
        for out, to in zip((m0, m1, m2, m3), (side, 1 - side, 2 + side, 3 - side)):
            plane = (row & 12) + to
            target = match(CAP_Z, ranks[3:4], (half == side) & (z_of == plane))
            out[...] = pick(joined(target, source), rows)


def spread_kernel(place, piv_ref, ranks_ref, m0, r1, r2, r3, d0, d1, d2, d3):
    row = place[0]

    @pl.when(row < ZN)
    def _():
        owner, local, x_of, z_of, half = unpack(piv_ref[...])
        ranks = ranks_ref[...]
        spot = row & 3
        first = jnp.where(spot < 2, m0[...], r2[...])
        second = jnp.where(spot < 2, r1[...], r3[...])
        rows = jnp.concatenate([first, second], axis=0)
        slot = ranks[3:4] + jnp.where(half == (spot & 1), 0, CAP_Z)
        source = match(2 * CAP_Z, slot)
        for x, out in enumerate((d0, d1, d2, d3)):
            target = match(CAP_OWN, ranks[0:1], owner == row + x * ZN)
            out[...] = pick(joined(target, source), rows)


def factor(place, top_ref, linv_ref, uinv_ref, w_ref, v_ref, upper_ref):
    row = place[0]
    w_ref[...] = jnp.zeros((NB, NB), F32)
    v_ref[...] = jnp.zeros((NB, NB), F32)
    upper_ref[...] = jnp.zeros((ROWS, NB), F32)
    eye = jnp.where(
        lax.broadcasted_iota(jnp.int32, (IB, IB), 0) == lax.broadcasted_iota(jnp.int32, (IB, IB), 1),
        F32(1.0),
        F32(0.0),
    )
    for block in range(BLOCKS):
        begin, end = block * IB, (block + 1) * IB
        linv, uinv = linv_ref[block], uinv_ref[block]
        upper = product(linv, top_ref[begin:end, begin:])

        @pl.when(row == begin // ROWS)
        def _():
            upper_ref[begin % ROWS : begin % ROWS + IB, begin:] = upper

        if begin:
            v_left = product(linv, v_ref[begin:end, :begin])
            v_ref[begin:end, :begin] = v_left
            w_up = product(w_ref[:begin, begin:end], uinv)
            w_ref[:begin, begin:end] = w_up
        v_ref[begin:end, begin:end] = linv
        w_ref[begin:end, begin:end] = uinv
        if end < NB:
            lower = product(top_ref[end:, begin:end], uinv)
            top_ref[end:, end:] -= product(lower, upper[:, IB:])
            v_ref[end:, :end] -= product(lower, v_ref[begin:end, :end])
            w_ref[:end, end:] -= product(w_ref[:end, begin:end], upper[:, IB:])


def order_kernel(place, cols_ref, a0, a1, a2, a3, linv, uinv, top_ref, w_ref, v_ref, upper_ref, work):
    row, col = place[0], place[1]
    cols = cols_ref[...]
    slot = (((row >> 4) - cols[:, 0:1]) & 3) * CAP_X + cols[:, 1:2]
    chosen = ones_at(lax.broadcasted_iota(jnp.int32, (NB, XN * CAP_X), 1) == slot)
    rows = jnp.concatenate([a0[...], a1[...], a2[...], a3[...]], axis=0)
    top = pick(chosen, rows)
    top_ref[...] = top

    @pl.when(col == 0)
    def _():
        work[...] = top
        factor(place, work, linv, uinv, w_ref, v_ref, upper_ref)


def factor_kernel(place, top_ref, linv, uinv, w_ref, v_ref, upper_ref, work):
    @pl.when(place[1] == 0)
    def _():
        work[...] = top_ref[...]
        factor(place, work, linv, uinv, w_ref, v_ref, upper_ref)


def placed(row, piv_ref, ranks_ref, mat_ref, d0, d1, d2, d3):
    owner, local, x_of, z_of, half = unpack(piv_ref[...])
    rows = jnp.where(row < ZN, d0[...], d1[...] + d2[...] + d3[...])
    mine = owner == row
    target = match(ROWS, local, mine)
    source = match(CAP_OWN, ranks_ref[0:1], mine)
    chosen = joined(target, source)
    hit = jnp.sum(chosen.astype(F32), axis=1, keepdims=True) > 0.5
    return jnp.where(hit, pick(chosen, rows), mat_ref[...])


def rows_kernel(moved, place, *refs):
    if moved:
        piv_ref, ranks_ref, mat_ref, d0, d1, d2, d3, w_ref, v_ref, upper_ref, q_ref, out_ref = refs
    else:
        mat_ref, w_ref, v_ref, upper_ref, q_ref, out_ref = refs
    row, col = place[0], place[1]

    @pl.when((col == 0) & (row < 2))
    def _():
        q_ref[...] = -jnp.where(row == 0, v_ref[:ROWS], v_ref[ROWS:])
        out_ref[...] = upper_ref[...]

    @pl.when((col == 0) & (row >= 2))
    def _():
        if moved:
            rows = placed(row, piv_ref, ranks_ref, mat_ref, d0, d1, d2, d3)
        else:
            rows = mat_ref[...]
        lower = product(rows, w_ref[...])
        out_ref[...] = lower
        q_ref[...] = product(lower, v_ref[...])


def final_kernel(moved, place, *refs):
    if moved:
        piv_ref, ranks_ref, mat_ref, d0, d1, d2, d3, q_ref, top_ref, panel_ref, out_ref = refs
    else:
        mat_ref, q_ref, top_ref, panel_ref, out_ref = refs
    row, col = place[0], place[1]

    @pl.when(col == 0)
    def _():
        out_ref[...] = panel_ref[...]

    @pl.when(col != 0)
    def _():
        change = product(q_ref[...], top_ref[...])
        if moved:
            rows = placed(row, piv_ref, ranks_ref, mat_ref, d0, d1, d2, d3)
        else:
            rows = mat_ref[...]
        out_ref[...] = jnp.where(row < 2, F32(0.0), rows) - change


def shape(rows, cols=NB, dtype=F32):
    return jax.ShapeDtypeStruct((rows, cols), dtype)


def call(kernel, out_shape, *args, scratch=(), out_specs=None):
    if out_specs is None:
        out_specs = jax.tree.map(lambda _: VMEM, out_shape)
    return pl.pallas_call(
        kernel,
        out_shape=out_shape,
        in_specs=[SMEM] + [VMEM] * (len(args) - 1),
        out_specs=out_specs,
        scratch_shapes=list(scratch),
        compiler_params=PARAMS,
    )(*args)


def shift_x(array, by):
    return lax.ppermute(array, "prow", [(i, (i + by * ZN) % (XN * ZN)) for i in range(XN * ZN)])


def broadcast(q):
    col = lax.axis_index("pcol")
    parts = [lax.ppermute(q, "pcol", [(0, to)]) for to in (4, 2, 6)]
    even = jnp.where(col == 0, q, parts[0] + parts[1] + parts[2])
    odd = lax.ppermute(even, "pcol", [(0, 1), (2, 3), (4, 5), (6, 7)])
    return jnp.where(col % 2 == 0, even, odd)


Z_RINGS = [[x * ZN + z for z in range(ZN)] for x in range(XN)]
PAIRS = [(4 * a, 4 * a + 1) for a in range(4)]
NEAR = [
    [(i, j) for i, j in PAIRS] + [(j, i) for i, j in PAIRS],
    [(i, i + 2) for i, j in PAIRS] + [(j, j + 2) for i, j in PAIRS],
    [(i, i + 3) for i, j in PAIRS] + [(j, j + 1) for i, j in PAIRS],
]


def direct(place, matrix, pivots, lower_inv, upper_inv, ranks, cols, asend, dmsg):
    far = [
        lax.ppermute(dmsg[a * CAP_ZB : (a + 1) * CAP_ZB], "prow", [(0, 4 * a), (1, 4 * a + 1)])
        for a in (1, 2, 3)
    ]
    gathered = lax.all_gather(asend, "prow", axis_index_groups=Z_RINGS, tiled=True)
    mine = call(group_kernel, shape(CAP_X), place, pivots, ranks, gathered)
    others = [shift_x(mine, by) for by in (1, 2, 3)]
    messages = call(near_kernel, [shape(CAP_Z)] * 4, place, pivots, ranks, dmsg, *far)
    near = [lax.ppermute(m, "prow", pairs) for m, pairs in zip(messages[1:], NEAR)]
    spread = call(spread_kernel, [shape(CAP_OWN)] * 4, place, pivots, ranks, messages[0], *near)
    moved = [spread[0]] + [
        lax.ppermute(spread[x], "prow", [(z, x * ZN + z) for z in range(ZN)]) for x in (1, 2, 3)
    ]
    top, w, v, upper = call(
        order_kernel,
        [shape(NB), shape(NB), shape(NB), shape(ROWS)],
        place, cols, mine, *others, lower_inv, upper_inv,
        scratch=[pltpu.VMEM((NB, NB), F32)],
    )
    q, panel = call(
        functools.partial(rows_kernel, True), [shape(ROWS)] * 2,
        place, pivots, ranks, matrix, *moved, w, v, upper,
    )
    q = broadcast(q)
    return call(
        functools.partial(final_kernel, True), shape(ROWS),
        place, pivots, ranks, matrix, *moved, q, top, panel,
    )


def general(place, matrix, pivots, lower_inv, upper_inv, ranks, cols, asend, dmsg):
    row = place[0]
    pivots = pivots[0]
    here = (pivots >> 8) == row
    local = pivots & 255
    index = jnp.arange(NB, dtype=jnp.int32)
    top_here = (index >> 8) == row
    both = jnp.concatenate(
        [
            jnp.where(here[:, None], matrix[local], F32(0.0)),
            jnp.where(top_here[:, None], matrix[index & 255], F32(0.0)),
        ],
        axis=0,
    )
    for bit in (1, 2, 4, 8, 16, 32):
        both = both + lax.ppermute(both, "prow", [(i, i ^ bit) for i in range(XN * ZN)])
    top, old = both[:NB], both[NB:]
    swapped = matrix.at[jnp.where(here, local, ROWS)].set(old, mode="drop")
    w, v, upper = call(
        factor_kernel, [shape(NB), shape(NB), shape(ROWS)],
        place, top, lower_inv, upper_inv,
        scratch=[pltpu.VMEM((NB, NB), F32)],
    )
    q, panel = call(
        functools.partial(rows_kernel, False), [shape(ROWS)] * 2, place, swapped, w, v, upper
    )
    q = broadcast(q)
    return call(functools.partial(final_kernel, False), shape(ROWS), place, swapped, q, top, panel)


def per_device(matrix, pivots, lower_inv, upper_inv):
    place = jnp.stack([lax.axis_index("prow"), lax.axis_index("pcol")]).astype(jnp.int32)
    pivots = pivots.reshape(1, NB)
    ranks, cols, asend, dmsg, fits = call(
        prep_kernel,
        [
            shape(8, NB, jnp.int32), shape(NB, 8, jnp.int32), shape(CAP_OWN), shape(4 * CAP_ZB),
            jax.ShapeDtypeStruct((1,), jnp.int32),
        ],
        place, pivots, matrix,
        out_specs=[VMEM, VMEM, VMEM, VMEM, SMEM],
    )
    return lax.cond(
        fits[0] == 1, direct, general,
        place, matrix, pivots, lower_inv, upper_inv, ranks, cols, asend, dmsg,
    )


def solution(mesh):
    in_specs = (P("prow", "pcol"), P(), P(), P())
    out_specs = P("prow", "pcol")
    return jax.shard_map(
        per_device, mesh=mesh, in_specs=in_specs, out_specs=out_specs, check_vma=False
    )
```

```python
import functools

import jax
import jax.numpy as jnp
from jax import lax
from jax.experimental import pallas as pl
from jax.experimental.pallas import tpu as pltpu
from jax.sharding import PartitionSpec as P

ROWS = 256
NB = 512
IB = 128
BLOCKS = NB // IB
XN = 4
ZN = 16
CAP_OWN = 24
CAP_X = 176
CAP_SX = 96
CAP_SXB = 40
CAP_SO = 16
PANEL = 1

VMEM = pl.BlockSpec(memory_space=pltpu.VMEM)
SMEM = pl.BlockSpec(memory_space=pltpu.SMEM)
ANY = pl.BlockSpec(memory_space=pl.ANY)
PARAMS = pltpu.CompilerParams(vmem_limit_bytes=48 * 1024 * 1024)
F32 = jnp.float32
BF16 = jnp.bfloat16


def two_parts(values):
    high = values.astype(BF16)
    return high, (values - high.astype(F32)).astype(BF16)


def product(left, right):
    left, left_low = two_parts(left)
    right, right_low = two_parts(right)
    small = jnp.dot(left, right_low, preferred_element_type=F32) + jnp.dot(
        left_low, right, preferred_element_type=F32
    )
    return jnp.dot(left, right, preferred_element_type=F32) + small


def exact_parts(values):
    high = values.astype(BF16)
    rest = values - high.astype(F32)
    middle = rest.astype(BF16)
    low = (rest - middle.astype(F32)).astype(BF16)
    return high, middle, low


def pick(chosen, values):
    high, middle, low = exact_parts(values)
    small = jnp.dot(chosen, middle, preferred_element_type=F32) + jnp.dot(
        chosen, low, preferred_element_type=F32
    )
    return jnp.dot(chosen, high, preferred_element_type=F32) + small


def ones_at(condition):
    return jnp.where(condition, F32(1.0), F32(0.0)).astype(BF16)


def match(slots, key, mask=None):
    rows = lax.broadcasted_iota(jnp.int32, (slots, key.shape[1]), 0)
    if mask is not None:
        key = jnp.where(mask, key, -1)
    return ones_at(rows == key)


def joined(target, source):
    both = lax.dot_general(target, source, (((1,), (1,)), ((), ())), preferred_element_type=F32)
    return both.astype(BF16)


def unpack(pivots):
    owner = pivots >> 8
    index = lax.broadcasted_iota(jnp.int32, pivots.shape, 1)
    return owner, pivots & 255, owner >> 4, owner & 15, index >> 8


def ranks_kernel(piv_ref, ranks_ref, cols_ref, ok_ref):
    owner, local, x_of, z_of, half = unpack(piv_ref[...])
    block = z_of >> 2
    keys = (
        (64, owner),
        (16, x_of),
        (16, half * 4 + x_of),
        (32, half * 16 + x_of * 4 + block),
        (128, half * 64 + owner),
    )
    classes = jnp.concatenate([match(count, key) for count, key in keys], axis=0)
    before = ones_at(
        lax.broadcasted_iota(jnp.int32, (NB, NB), 0) < lax.broadcasted_iota(jnp.int32, (NB, NB), 1)
    )
    counts = jnp.dot(classes, before, preferred_element_type=F32) * classes.astype(F32)
    ranks, start = [], 0
    for count, _ in keys:
        ranks.append(jnp.sum(counts[start : start + count], axis=0, keepdims=True))
        start += count
    fits = jnp.max(ranks[0]) < CAP_OWN
    for rank, cap in zip(ranks[1:], (CAP_X, CAP_SX, CAP_SXB, CAP_SO)):
        fits = fits & (jnp.max(rank) < cap)
    ok_ref[0] = jnp.where(fits, 1, 0).astype(jnp.int32)
    zero = jnp.zeros_like(ranks[0])
    ranks_ref[...] = jnp.concatenate(ranks + [zero] * 3, axis=0).astype(jnp.int32)
    wanted = jnp.concatenate(
        [x_of.astype(F32), jnp.minimum(ranks[1], 255.0)] + [zero] * 6, axis=0
    ).astype(BF16)
    diagonal = ones_at(
        lax.broadcasted_iota(jnp.int32, (NB, NB), 0) == lax.broadcasted_iota(jnp.int32, (NB, NB), 1)
    )
    cols_ref[...] = lax.dot_general(
        diagonal, wanted, (((1,), (1,)), ((), ())), preferred_element_type=F32
    ).astype(jnp.int32)


def pack_kernel(place, piv_ref, ranks_ref, mat_ref, asend_ref, m0, m1, m2, m3):
    row = place[0]
    owner, local, x_of, z_of, half = unpack(piv_ref[...])
    ranks = ranks_ref[...]
    chosen = joined(match(CAP_OWN, ranks[0:1], owner == row), match(ROWS, local))
    asend_ref[...] = pick(chosen, mat_ref[...])

    @pl.when(row < 2)
    def _():
        rank = jnp.where(row == 0, ranks[2:3, :ROWS], ranks[2:3, ROWS:])
        to = jnp.where(row == 0, x_of[:, :ROWS], x_of[:, ROWS:])
        chosen = jnp.concatenate([match(CAP_SX, rank, to == x) for x in range(XN)], axis=0)
        picked = pick(chosen, mat_ref[...])
        for x, out in enumerate((m0, m1, m2, m3)):
            out[...] = picked[x * CAP_SX : (x + 1) * CAP_SX]


def group_kernel(place, piv_ref, ranks_ref, gathered_ref, amsg_ref):
    row = place[0]
    owner, local, x_of, z_of, half = unpack(piv_ref[...])
    ranks = ranks_ref[...]
    target = match(CAP_X, ranks[1:2], x_of == (row >> 4))
    source = match(ZN * CAP_OWN, z_of * CAP_OWN + ranks[0:1])
    amsg_ref[...] = pick(joined(target, source), gathered_ref[...])


def far_kernel(place, piv_ref, ranks_ref, here_ref, r1, r2, r3, m0, m1, m2, m3):
    row = place[0]

    @pl.when((row & 15) < 2)
    def _():
        owner, local, x_of, z_of, half = unpack(piv_ref[...])
        ranks = ranks_ref[...]
        rows = jnp.where(row < 2, here_ref[...], r1[...] + r2[...] + r3[...])
        mine = (half == (row & 1)) & (x_of == (row >> 4))
        source = match(CAP_SX, ranks[2:3])
        target = jnp.concatenate(
            [match(CAP_SXB, ranks[3:4], mine & ((z_of >> 2) == block)) for block in range(4)], axis=0
        )
        picked = pick(joined(target, source), rows)
        for block, out in enumerate((m0, m1, m2, m3)):
            out[...] = picked[block * CAP_SXB : (block + 1) * CAP_SXB]


def near_kernel(place, piv_ref, ranks_ref, r0, r1, r2, r3, m0, m1, m2, m3):
    row = place[0]

    @pl.when((row & 3) >= 2)
    def _():
        owner, local, x_of, z_of, half = unpack(piv_ref[...])
        ranks = ranks_ref[...]
        side = row & 1
        rows = (r0[...] + r1[...]) + (r2[...] + r3[...])
        source = match(CAP_SXB, ranks[3:4])
        target = jnp.concatenate(
            [
                match(CAP_SO, ranks[4:5], (half == side) & (owner == (row & 60) + to))
                for to in (2 + side, 3 - side, side, 1 - side)
            ],
            axis=0,
        )
        picked = pick(joined(target, source), rows)
        for at, out in enumerate((m0, m1, m2, m3)):
            out[...] = picked[at * CAP_SO : (at + 1) * CAP_SO]


def factor(place, top_ref, linv_ref, uinv_ref, w_ref, v_ref, upper_ref):
    row = place[0]
    w_ref[...] = jnp.zeros((NB, NB), F32)
    v_ref[...] = jnp.zeros((NB, NB), F32)
    upper_ref[...] = jnp.zeros((ROWS, NB), F32)
    eye = jnp.where(
        lax.broadcasted_iota(jnp.int32, (IB, IB), 0) == lax.broadcasted_iota(jnp.int32, (IB, IB), 1),
        F32(1.0),
        F32(0.0),
    )
    for block in range(BLOCKS):
        begin, end = block * IB, (block + 1) * IB
        linv, uinv = linv_ref[block], uinv_ref[block]
        upper = product(linv, top_ref[begin:end, begin:])

        @pl.when(row == begin // ROWS)
        def _():
            upper_ref[begin % ROWS : begin % ROWS + IB, begin:] = upper

        if begin:
            v_left = product(linv, v_ref[begin:end, :begin])
            v_ref[begin:end, :begin] = v_left
            w_up = product(w_ref[:begin, begin:end], uinv)
            w_ref[:begin, begin:end] = w_up
        v_ref[begin:end, begin:end] = linv
        w_ref[begin:end, begin:end] = uinv
        if end < NB:
            lower = product(top_ref[end:, begin:end], uinv)
            top_ref[end:, end:] -= product(lower, upper[:, IB:])
            v_ref[end:, :end] -= product(lower, v_ref[begin:end, :end])
            w_ref[:end, end:] -= product(w_ref[:end, begin:end], upper[:, IB:])


def order_kernel(place, cols_ref, a0, a1, a2, a3, linv, uinv, top_ref, w_ref, v_ref, upper_ref, work):
    cols = cols_ref[...]
    slot = (((place[0] >> 4) - cols[:, 0:1]) & 3) * CAP_X + cols[:, 1:2]
    chosen = ones_at(lax.broadcasted_iota(jnp.int32, (NB, XN * CAP_X), 1) == slot)
    rows = jnp.concatenate([a0[...], a1[...], a2[...], a3[...]], axis=0)
    top = pick(chosen, rows)
    top_ref[...] = top

    @pl.when(place[1] == PANEL)
    def _():
        work[...] = top
        factor(place, work, linv, uinv, w_ref, v_ref, upper_ref)


def factor_kernel(place, top_ref, linv, uinv, w_ref, v_ref, upper_ref, work):
    @pl.when(place[1] == PANEL)
    def _():
        work[...] = top_ref[...]
        factor(place, work, linv, uinv, w_ref, v_ref, upper_ref)


def placed(row, piv_ref, ranks_ref, mat_ref, old):
    owner, local, x_of, z_of, half = unpack(piv_ref[...])
    mine = owner == row
    slot = ranks_ref[4:5] + jnp.where(half == (row & 1), 0, CAP_SO)
    chosen = joined(match(ROWS, local, mine), match(2 * CAP_SO, slot, mine))
    hit = jnp.sum(chosen.astype(F32), axis=1, keepdims=True) > 0.5
    return jnp.where(hit, pick(chosen, old), mat_ref[...])


def rows_kernel(moved, place, *refs):
    if moved:
        (piv_ref, ranks_ref, mat_ref, m0, r1, r2, r3, top_ref, w_ref, v_ref, upper_ref,
         qa_ref, qb_ref, qc_ref, panel_ref, old_ref) = refs
    else:
        mat_ref, top_ref, w_ref, v_ref, upper_ref, qa_ref, qb_ref, qc_ref, panel_ref = refs
    row, col = place[0], place[1]
    if moved:
        spot = row & 3
        old_ref[:CAP_SO] = jnp.where(spot >= 2, m0[...], r2[...])
        old_ref[CAP_SO:] = jnp.where(spot >= 2, r1[...], r3[...])

    @pl.when(col == 0)
    def _():
        qa_ref[...] = top_ref[:ROWS]
        qb_ref[...] = top_ref[ROWS:]
        if moved:
            qc_ref[: 2 * CAP_SO] = old_ref[...]
        else:
            qc_ref[...] = mat_ref[...]

    @pl.when((col == PANEL) & (row < 2))
    def _():
        q = -jnp.where(row == 0, v_ref[:ROWS], v_ref[ROWS:])
        for q_ref in (qa_ref, qb_ref, qc_ref):
            q_ref[...] = q
        panel_ref[...] = upper_ref[...]

    @pl.when((col == PANEL) & (row >= 2))
    def _():
        if moved:
            rows = placed(row, piv_ref, ranks_ref, mat_ref, old_ref[...])
        else:
            rows = mat_ref[...]
        half = NB // 2
        left = product(rows[:, :half], w_ref[:half, :half])
        right = product(rows, w_ref[:, half:])
        panel_ref[:, :half] = left
        panel_ref[:, half:] = right
        q_left = product(left, v_ref[:half, :half]) + product(right, v_ref[half:, :half])
        q_right = product(right, v_ref[half:, half:])
        for q_ref in (qa_ref, qb_ref, qc_ref):
            q_ref[:, :half] = q_left
            q_ref[:, half:] = q_right


def base_rows(moved, row, refs, more):
    rows = placed(row, *refs, more) if moved else more
    return jnp.where(row < 2, F32(0.0), rows)


def ready_kernel(moved, place, *refs):
    *rows_refs, more_ref, top_ref, base_ref, high_ref, low_ref = refs

    @pl.when(place[1] > 1)
    def _():
        base_ref[...] = base_rows(moved, place[0], rows_refs, more_ref[...])
        high_ref[...], low_ref[...] = two_parts(top_ref[...])


def final_kernel(moved, place, *refs):
    if moved:
        *rows_refs, out_ref, q_buf = refs
        rows_refs, refs = rows_refs[:3], (*rows_refs[3:], out_ref, q_buf)
    else:
        rows_refs = ()
    base_ref, high_ref, low_ref, panel_ref, *q_refs, out_ref, q_buf = refs
    row, col = place[0], place[1]

    @pl.when(col == 0)
    def _():
        out_ref[...] = panel_ref[...]

    for source, q_ref in zip((5, 3, 7, 4, 2, 6), q_refs[1:]):

        @pl.when(col == source)
        def _():
            q_buf[...] = q_ref[...]

    @pl.when(col == 1)
    def _():
        first, second, third = q_refs[1:4]
        more = third[: 2 * CAP_SO] if moved else third[...]
        q = q_refs[0][...]
        change = product(q[:, :ROWS], first[...]) + product(q[:, ROWS:], second[...])
        out_ref[...] = base_rows(moved, row, rows_refs, more) - change

    @pl.when(col > 1)
    def _():
        top = high_ref[...]
        q, q_low = two_parts(q_buf[...])
        change = jnp.dot(q, top, preferred_element_type=F32) + (
            jnp.dot(q, low_ref[...], preferred_element_type=F32)
            + jnp.dot(q_low, top, preferred_element_type=F32)
        )
        out_ref[...] = base_ref[...] - change


def shape(rows, cols=NB, dtype=F32):
    return jax.ShapeDtypeStruct((rows, cols), dtype)


def call(kernel, out_shape, *args, scratch=(), in_specs=None, out_specs=None):
    if in_specs is None:
        in_specs = [SMEM] + [VMEM] * (len(args) - 1)
    if out_specs is None:
        out_specs = jax.tree.map(lambda _: VMEM, out_shape)
    return pl.pallas_call(
        kernel,
        out_shape=out_shape,
        in_specs=in_specs,
        out_specs=out_specs,
        scratch_shapes=list(scratch),
        compiler_params=PARAMS,
    )(*args)


def shift_x(array, by):
    return lax.ppermute(array, "prow", [(i, (i + by * ZN) % (XN * ZN)) for i in range(XN * ZN)])


def swap_blocks(array):
    return lax.ppermute(array, "pcol", [(0, 1), (1, 0)] + [(k, k) for k in range(2, 8)])


def finish(moved, place, args, more, top, panel, messages):
    parts = [
        lax.ppermute(m, "pcol", [(PANEL, to), (0, PANEL)]) for m, to in zip(messages, (5, 3, 7))
    ]
    ready = call(
        functools.partial(ready_kernel, moved), [shape(ROWS), shape(NB, NB, BF16), shape(NB, NB, BF16)],
        place, *args, more, top,
    )
    first, ready = lax.optimization_barrier((parts[0], ready))
    hops = [
        lax.ppermute(part, "pcol", [(of, of - 1)])
        for part, of in zip((first, *parts[1:]), (5, 3, 7))
    ]
    panel, _ = lax.optimization_barrier((panel, first))
    panel = lax.ppermute(panel, "pcol", [(PANEL, 0)])
    return call(
        functools.partial(final_kernel, moved), shape(ROWS),
        place, *args, *ready, panel, messages[0], *parts, *hops,
        scratch=[pltpu.VMEM((ROWS, NB), F32)],
    )


Z_RINGS = [[x * ZN + z for z in range(ZN)] for x in range(XN)]
PAIRS = [(4 * a + 2, 4 * a + 3) for a in range(XN * ZN // 4)]
NEAR = [
    [(i, j) for i, j in PAIRS] + [(j, i) for i, j in PAIRS],
    [(i, i - 2) for i, j in PAIRS] + [(j, j - 2) for i, j in PAIRS],
    [(i, i - 1) for i, j in PAIRS] + [(j, j - 3) for i, j in PAIRS],
]


def direct(place, matrix, work, pivots, lower_inv, upper_inv, ranks, cols):
    asend, *old = call(
        pack_kernel, [shape(CAP_OWN)] + [shape(CAP_SX)] * 4, place, pivots, ranks, work
    )
    to_x = [
        lax.ppermute(old[x], "prow", [(s, x * ZN + s) for s in (0, 1)]) for x in (1, 3, 2)
    ]
    gathered = lax.all_gather(asend, "prow", axis_index_groups=Z_RINGS, tiled=True)
    gathered, old[0], to_x = lax.optimization_barrier((gathered, old[0], to_x))
    old = call(far_kernel, [shape(CAP_SXB)] * 4, place, pivots, ranks, old[0], *to_x)
    gathered, old = lax.optimization_barrier((gathered, old))
    to_block = [
        lax.ppermute(
            old[a], "prow", [(x * ZN + s, x * ZN + 4 * a + 2 + s) for x in range(XN) for s in (0, 1)]
        )
        for a in (0, 3, 1, 2)
    ]
    mine = call(group_kernel, shape(CAP_X), place, pivots, ranks, gathered)
    others = [shift_x(mine, by) for by in (1, 2, 3)]
    old = call(near_kernel, [shape(CAP_SO)] * 4, place, pivots, ranks, *to_block)
    near = [lax.ppermute(m, "prow", pairs) for m, pairs in zip(old[1:], NEAR)]
    top, w, v, upper = call(
        order_kernel, [shape(NB), shape(NB), shape(NB), shape(ROWS)],
        place, cols, mine, *others, lower_inv, upper_inv,
        scratch=[pltpu.VMEM((NB, NB), F32)],
    )
    *messages, panel, old = call(
        functools.partial(rows_kernel, True), [shape(ROWS)] * 4 + [shape(2 * CAP_SO)],
        place, pivots, ranks, work, old[0], *near, top, w, v, upper,
    )
    return finish(True, place, (pivots, ranks, matrix), old, top, panel, messages)


def general(place, matrix, work, pivots, lower_inv, upper_inv, ranks, cols):
    row = place[0]
    pivots = pivots[0]
    here = (pivots >> 8) == row
    local = pivots & 255
    index = jnp.arange(NB, dtype=jnp.int32)
    top_here = (index >> 8) == row
    both = jnp.concatenate(
        [
            jnp.where(here[:, None], work[local], F32(0.0)),
            jnp.where(top_here[:, None], work[index & 255], F32(0.0)),
        ],
        axis=0,
    )
    for bit in (1, 2, 4, 8, 16, 32):
        both = both + lax.ppermute(both, "prow", [(i, i ^ bit) for i in range(XN * ZN)])
    top, old = both[:NB], both[NB:]
    swapped = work.at[jnp.where(here, local, ROWS)].set(old, mode="drop")
    w, v, upper = call(
        factor_kernel, [shape(NB), shape(NB), shape(ROWS)],
        place, top, lower_inv, upper_inv,
        scratch=[pltpu.VMEM((NB, NB), F32)],
    )
    *messages, panel = call(
        functools.partial(rows_kernel, False), [shape(ROWS)] * 4,
        place, swapped, top, w, v, upper,
    )
    return finish(False, place, (), swapped, top, panel, messages)


def per_device(matrix, pivots, lower_inv, upper_inv):
    place = jnp.stack([lax.axis_index("prow"), lax.axis_index("pcol")]).astype(jnp.int32)
    pivots = pivots.reshape(1, NB)
    work = swap_blocks(matrix)
    ranks, cols, fits = call(
        ranks_kernel,
        [shape(8, NB, jnp.int32), shape(NB, 8, jnp.int32), jax.ShapeDtypeStruct((1,), jnp.int32)],
        pivots,
        in_specs=[VMEM],
        out_specs=[VMEM, VMEM, SMEM],
    )
    return lax.cond(
        fits[0] == 1, direct, general,
        place, matrix, work, pivots, lower_inv, upper_inv, ranks, cols,
    )


def solution(mesh):
    in_specs = (P("prow", "pcol"), P(), P(), P())
    out_specs = P("prow", "pcol")
    return jax.shard_map(
        per_device, mesh=mesh, in_specs=in_specs, out_specs=out_specs, check_vma=False
    )
```

```python
import functools

import jax
import jax.numpy as jnp
from jax import lax
from jax.experimental import pallas as pl
from jax.experimental.pallas import tpu as pltpu
from jax.sharding import PartitionSpec as P

ROWS = 256
NB = 512
IB = 128
BLOCKS = NB // IB
XN = 4
ZN = 16
CAP_OWN = 24
CAP_X = 176
CAP_SX = 96
CAP_SXB = 40
CAP_SO = 16
PANEL = 1

VMEM = pl.BlockSpec(memory_space=pltpu.VMEM)
SMEM = pl.BlockSpec(memory_space=pltpu.SMEM)
ANY = pl.BlockSpec(memory_space=pl.ANY)
PARAMS = pltpu.CompilerParams(vmem_limit_bytes=48 * 1024 * 1024)
F32 = jnp.float32
BF16 = jnp.bfloat16


def two_parts(values):
    high = values.astype(BF16)
    return high, (values - high.astype(F32)).astype(BF16)


def product(left, right):
    left, left_low = two_parts(left)
    right, right_low = two_parts(right)
    small = jnp.dot(left, right_low, preferred_element_type=F32) + jnp.dot(
        left_low, right, preferred_element_type=F32
    )
    return jnp.dot(left, right, preferred_element_type=F32) + small


def exact_parts(values):
    high = values.astype(BF16)
    rest = values - high.astype(F32)
    middle = rest.astype(BF16)
    low = (rest - middle.astype(F32)).astype(BF16)
    return high, middle, low


def pick(chosen, values):
    high, middle, low = exact_parts(values)
    small = jnp.dot(chosen, middle, preferred_element_type=F32) + jnp.dot(
        chosen, low, preferred_element_type=F32
    )
    return jnp.dot(chosen, high, preferred_element_type=F32) + small


def ones_at(condition):
    return jnp.where(condition, F32(1.0), F32(0.0)).astype(BF16)


def match(slots, key, mask=None):
    rows = lax.broadcasted_iota(jnp.int32, (slots, key.shape[1]), 0)
    if mask is not None:
        key = jnp.where(mask, key, -1)
    return ones_at(rows == key)


def joined(target, source):
    both = lax.dot_general(target, source, (((1,), (1,)), ((), ())), preferred_element_type=F32)
    return both.astype(BF16)


def unpack(pivots):
    owner = pivots >> 8
    index = lax.broadcasted_iota(jnp.int32, pivots.shape, 1)
    return owner, pivots & 255, owner >> 4, owner & 15, index >> 8


def ranks_kernel(piv_ref, ranks_ref, cols_ref, ok_ref):
    owner, local, x_of, z_of, half = unpack(piv_ref[...])
    block = z_of >> 2
    keys = (
        (64, owner),
        (16, x_of),
        (16, half * 4 + x_of),
        (32, half * 16 + x_of * 4 + block),
        (128, half * 64 + owner),
    )
    classes = jnp.concatenate([match(count, key) for count, key in keys], axis=0)
    rows = lax.broadcasted_iota(jnp.int32, (IB, 2 * IB), 0)
    lanes = lax.broadcasted_iota(jnp.int32, (IB, 2 * IB), 1)
    counter = ones_at((rows < lanes) | (lanes >= IB))
    passed, pieces = jnp.zeros((classes.shape[0], IB), F32), []
    for block in range(BLOCKS):
        held = classes[:, block * IB : (block + 1) * IB]
        count = jnp.dot(held, counter, preferred_element_type=F32)
        counts = (count[:, :IB] + passed) * held.astype(F32)
        passed = passed + count[:, IB:]
        start, piece = 0, []
        for size, _ in keys:
            piece.append(jnp.sum(counts[start : start + size], axis=0, keepdims=True))
            start += size
        pieces.append(jnp.concatenate(piece + [jnp.zeros((3, IB), F32)], axis=0))
    ranks = jnp.concatenate(pieces, axis=1)
    fits = jnp.max(ranks[0:1]) < CAP_OWN
    for at, cap in enumerate((CAP_X, CAP_SX, CAP_SXB, CAP_SO)):
        fits = fits & (jnp.max(ranks[at + 1 : at + 2]) < cap)
    ok_ref[0] = jnp.where(fits, 1, 0).astype(jnp.int32)
    ranks_ref[...] = ranks.astype(jnp.int32)
    zero = jnp.zeros((6, NB), F32)
    wanted = jnp.concatenate(
        [x_of.astype(F32), jnp.minimum(ranks[1:2], 255.0), zero], axis=0
    ).astype(BF16)
    diagonal = ones_at(rows[:, :IB] == lanes[:, :IB])
    for block in range(BLOCKS):
        part = slice(block * IB, (block + 1) * IB)
        cols_ref[part] = lax.dot_general(
            diagonal, wanted[:, part], (((1,), (1,)), ((), ())), preferred_element_type=F32
        ).astype(jnp.int32)


def pack_kernel(place, piv_ref, ranks_ref, mat_ref, asend_ref, m0, m1, m2, m3):
    row = place[0]
    owner, local, x_of, z_of, half = unpack(piv_ref[...])
    ranks = ranks_ref[...]
    chosen = joined(match(CAP_OWN, ranks[0:1], owner == row), match(ROWS, local))
    asend_ref[...] = pick(chosen, mat_ref[...])

    @pl.when(row < 2)
    def _():
        rank = jnp.where(row == 0, ranks[2:3, :ROWS], ranks[2:3, ROWS:])
        to = jnp.where(row == 0, x_of[:, :ROWS], x_of[:, ROWS:])
        chosen = jnp.concatenate([match(CAP_SX, rank, to == x) for x in range(XN)], axis=0)
        picked = pick(chosen, mat_ref[...])
        for x, out in enumerate((m0, m1, m2, m3)):
            out[...] = picked[x * CAP_SX : (x + 1) * CAP_SX]


def group_kernel(
    place, piv_ref, ranks_ref, gathered_ref, here_ref, r1, r2, r3, amsg_ref, m0, m1, m2, m3
):
    row = place[0]
    owner, local, x_of, z_of, half = unpack(piv_ref[...])
    ranks = ranks_ref[...]
    in_x = x_of == (row >> 4)
    target = match(CAP_X, ranks[1:2], in_x)
    source = match(ZN * CAP_OWN, z_of * CAP_OWN + ranks[0:1])
    amsg_ref[...] = pick(joined(target, source), gathered_ref[...])

    @pl.when((row & 15) < 2)
    def _():
        rows = jnp.where(row < 2, here_ref[...], r1[...] + r2[...] + r3[...])
        mine = (half == (row & 1)) & in_x
        source = match(CAP_SX, ranks[2:3])
        target = jnp.concatenate(
            [match(CAP_SXB, ranks[3:4], mine & ((z_of >> 2) == block)) for block in range(4)], axis=0
        )
        picked = pick(joined(target, source), rows)
        for block, out in enumerate((m0, m1, m2, m3)):
            out[...] = picked[block * CAP_SXB : (block + 1) * CAP_SXB]


def near_kernel(place, piv_ref, ranks_ref, r0, r1, r2, r3, m0, m1, m2, m3):
    row = place[0]

    @pl.when((row & 3) >= 2)
    def _():
        owner, local, x_of, z_of, half = unpack(piv_ref[...])
        ranks = ranks_ref[...]
        side = row & 1
        rows = (r0[...] + r1[...]) + (r2[...] + r3[...])
        source = match(CAP_SXB, ranks[3:4])
        target = jnp.concatenate(
            [
                match(CAP_SO, ranks[4:5], (half == side) & (owner == (row & 60) + to))
                for to in (2 + side, 3 - side, side, 1 - side)
            ],
            axis=0,
        )
        picked = pick(joined(target, source), rows)
        for at, out in enumerate((m0, m1, m2, m3)):
            out[...] = picked[at * CAP_SO : (at + 1) * CAP_SO]


def factor(place, top_ref, linv_ref, uinv_ref, w_ref, v_ref, upper_ref):
    row = place[0]
    w_ref[...] = jnp.zeros((NB, NB), F32)
    v_ref[...] = jnp.zeros((NB, NB), F32)
    upper_ref[...] = jnp.zeros((ROWS, NB), F32)
    eye = jnp.where(
        lax.broadcasted_iota(jnp.int32, (IB, IB), 0) == lax.broadcasted_iota(jnp.int32, (IB, IB), 1),
        F32(1.0),
        F32(0.0),
    )
    for block in range(BLOCKS):
        begin, end = block * IB, (block + 1) * IB
        linv, uinv = linv_ref[block], uinv_ref[block]
        upper = product(linv, top_ref[begin:end, begin:])

        @pl.when(row == begin // ROWS)
        def _():
            upper_ref[begin % ROWS : begin % ROWS + IB, begin:] = upper

        if begin:
            v_left = product(linv, v_ref[begin:end, :begin])
            v_ref[begin:end, :begin] = v_left
            w_up = product(w_ref[:begin, begin:end], uinv)
            w_ref[:begin, begin:end] = w_up
        v_ref[begin:end, begin:end] = linv
        w_ref[begin:end, begin:end] = uinv
        if end < NB:
            lower = product(top_ref[end:, begin:end], uinv)
            top_ref[end:, end:] -= product(lower, upper[:, IB:])
            v_ref[end:, :end] -= product(lower, v_ref[begin:end, :end])
            w_ref[:end, end:] -= product(w_ref[:end, begin:end], upper[:, IB:])


def order_kernel(place, cols_ref, a0, a1, a2, a3, linv, uinv, top_ref, w_ref, v_ref, upper_ref, work):
    cols = cols_ref[...]
    slot = (((place[0] >> 4) - cols[:, 0:1]) & 3) * CAP_X + cols[:, 1:2]
    chosen = ones_at(lax.broadcasted_iota(jnp.int32, (NB, XN * CAP_X), 1) == slot)
    rows = jnp.concatenate([a0[...], a1[...], a2[...], a3[...]], axis=0)
    high, low = two_parts(rows)
    top = jnp.dot(chosen, high, preferred_element_type=F32) + jnp.dot(
        chosen, low, preferred_element_type=F32
    )
    top_ref[...] = top

    @pl.when(place[1] == PANEL)
    def _():
        work[...] = top
        factor(place, work, linv, uinv, w_ref, v_ref, upper_ref)


def factor_kernel(place, top_ref, linv, uinv, w_ref, v_ref, upper_ref, work):
    @pl.when(place[1] == PANEL)
    def _():
        work[...] = top_ref[...]
        factor(place, work, linv, uinv, w_ref, v_ref, upper_ref)


def placed(row, piv_ref, ranks_ref, mat_ref, old):
    owner, local, x_of, z_of, half = unpack(piv_ref[...])
    mine = owner == row
    slot = ranks_ref[4:5] + jnp.where(half == (row & 1), 0, CAP_SO)
    chosen = joined(match(ROWS, local, mine), match(2 * CAP_SO, slot, mine))
    hit = jnp.sum(chosen.astype(F32), axis=1, keepdims=True) > 0.5
    return jnp.where(hit, pick(chosen, old), mat_ref[...])


def rows_kernel(moved, place, *refs):
    if moved:
        (piv_ref, ranks_ref, mat_ref, m0, r1, r2, r3, w_ref, v_ref, upper_ref,
         q_ref, panel_ref, old_ref) = refs
    else:
        mat_ref, w_ref, v_ref, upper_ref, q_ref, panel_ref = refs
    row, col = place[0], place[1]
    if moved:
        spot = row & 3
        old_ref[:CAP_SO] = jnp.where(spot >= 2, m0[...], r2[...])
        old_ref[CAP_SO:] = jnp.where(spot >= 2, r1[...], r3[...])

    @pl.when(col == 0)
    def _():
        if moved:
            q_ref[: 2 * CAP_SO] = old_ref[...]
        else:
            q_ref[...] = mat_ref[...]

    @pl.when((col == PANEL) & (row < 2))
    def _():
        q_ref[...] = -jnp.where(row == 0, v_ref[:ROWS], v_ref[ROWS:])
        panel_ref[...] = upper_ref[...]

    @pl.when((col == PANEL) & (row >= 2))
    def _():
        if moved:
            rows = placed(row, piv_ref, ranks_ref, mat_ref, old_ref[...])
        else:
            rows = mat_ref[...]
        half = NB // 2
        left = product(rows[:, :half], w_ref[:half, :half])
        right = product(rows, w_ref[:, half:])
        panel_ref[:, :half] = left
        panel_ref[:, half:] = right
        q_ref[:, :half] = product(left, v_ref[:half, :half]) + product(right, v_ref[half:, :half])
        q_ref[:, half:] = product(right, v_ref[half:, half:])


def base_rows(moved, row, refs, more):
    rows = placed(row, *refs, more) if moved else more
    return jnp.where(row < 2, F32(0.0), rows)


def ready_kernel(moved, place, *refs):
    *rows_refs, more_ref, top_ref, base_ref, high_ref, low_ref = refs

    @pl.when(place[1] > 1)
    def _():
        base_ref[...] = base_rows(moved, place[0], rows_refs, more_ref[...])
        high_ref[...], low_ref[...] = two_parts(top_ref[...])


def pass_kernel(place, a_ref, b_ref, c_ref, panel_ref, out_ref):
    for source, ref in ((5, a_ref), (3, b_ref), (7, c_ref), (PANEL, panel_ref)):

        @pl.when(place[1] == source)
        def _():
            out_ref[...] = ref[...]


def final_kernel(moved, place, *refs):
    rows_refs, refs = refs[: 3 * moved], refs[3 * moved :]
    base_ref, high_ref, low_ref, top_ref, q_ref, a_ref, b_ref, c_ref, hop_ref, out_ref, q_buf = refs
    row, col = place[0], place[1]

    @pl.when(col == 0)
    def _():
        out_ref[...] = hop_ref[...]

    @pl.when(col == 1)
    def _():
        more = a_ref[: 2 * CAP_SO] if moved else a_ref[...]
        out_ref[...] = base_rows(moved, row, rows_refs, more) - product(q_ref[...], top_ref[...])

    for sources, ref in (((5,), a_ref), ((3,), b_ref), ((7,), c_ref), ((2, 4, 6), hop_ref)):

        @pl.when(functools.reduce(jnp.logical_or, [col == source for source in sources]))
        def _():
            q_buf[...] = ref[...]

    @pl.when(col > 1)
    def _():
        top = high_ref[...]
        q, q_low = two_parts(q_buf[...])
        change = jnp.dot(q, top, preferred_element_type=F32) + (
            jnp.dot(q, low_ref[...], preferred_element_type=F32)
            + jnp.dot(q_low, top, preferred_element_type=F32)
        )
        out_ref[...] = base_ref[...] - change


def shape(rows, cols=NB, dtype=F32):
    return jax.ShapeDtypeStruct((rows, cols), dtype)


def call(kernel, out_shape, *args, scratch=(), in_specs=None, out_specs=None):
    if in_specs is None:
        in_specs = [SMEM] + [VMEM] * (len(args) - 1)
    if out_specs is None:
        out_specs = jax.tree.map(lambda _: VMEM, out_shape)
    return pl.pallas_call(
        kernel,
        out_shape=out_shape,
        in_specs=in_specs,
        out_specs=out_specs,
        scratch_shapes=list(scratch),
        compiler_params=PARAMS,
    )(*args)


def shift_x(array, by):
    return lax.ppermute(array, "prow", [(i, (i + by * ZN) % (XN * ZN)) for i in range(XN * ZN)])


def swap_blocks(array):
    return lax.ppermute(array, "pcol", [(0, 1), (1, 0)] + [(k, k) for k in range(2, 8)])


def finish(moved, place, args, more, top, panel, message):
    top_moved = lax.ppermute(top, "pcol", [(0, PANEL)])
    parts = [
        lax.ppermute(message, "pcol", pairs)
        for pairs in ([(PANEL, 5), (0, PANEL)], [(PANEL, 3)], [(PANEL, 7)])
    ]
    ready = call(
        functools.partial(ready_kernel, moved), [shape(ROWS), shape(NB, NB, BF16), shape(NB, NB, BF16)],
        place, *args, more, top,
    )
    parts, ready = lax.optimization_barrier((parts, ready))
    onward = call(pass_kernel, shape(ROWS), place, *parts, panel)
    hop = lax.ppermute(onward, "pcol", [(5, 4), (3, 2), (7, 6), (PANEL, 0)])
    return call(
        functools.partial(final_kernel, moved), shape(ROWS),
        place, *args, *ready, top_moved, message, *parts, hop,
        scratch=[pltpu.VMEM((ROWS, NB), F32)],
    )


Z_RINGS = [[x * ZN + z for z in range(ZN)] for x in range(XN)]
PAIRS = [(4 * a + 2, 4 * a + 3) for a in range(XN * ZN // 4)]
NEAR = [
    [(i, j) for i, j in PAIRS] + [(j, i) for i, j in PAIRS],
    [(i, i - 2) for i, j in PAIRS] + [(j, j - 2) for i, j in PAIRS],
    [(i, i - 1) for i, j in PAIRS] + [(j, j - 3) for i, j in PAIRS],
]


def direct(place, matrix, work, pivots, lower_inv, upper_inv, ranks, cols):
    asend, *old = call(
        pack_kernel, [shape(CAP_OWN)] + [shape(CAP_SX)] * 4, place, pivots, ranks, work
    )
    to_x = [
        lax.ppermute(old[x], "prow", [(s, x * ZN + s) for s in (0, 1)]) for x in (1, 3, 2)
    ]
    gathered = lax.all_gather(asend, "prow", axis_index_groups=Z_RINGS, tiled=True)
    mine, *old = call(
        group_kernel, [shape(CAP_X)] + [shape(CAP_SXB)] * 4,
        place, pivots, ranks, gathered, old[0], *to_x,
    )
    to_block = [
        lax.ppermute(
            old[a], "prow", [(x * ZN + s, x * ZN + 4 * a + 2 + s) for x in range(XN) for s in (0, 1)]
        )
        for a in (0, 3, 1, 2)
    ]
    others = [shift_x(mine, by) for by in (1, 2, 3)]
    old = call(near_kernel, [shape(CAP_SO)] * 4, place, pivots, ranks, *to_block)
    near = [lax.ppermute(m, "prow", pairs) for m, pairs in zip(old[1:], NEAR)]
    top, w, v, upper = call(
        order_kernel, [shape(NB), shape(NB), shape(NB), shape(ROWS)],
        place, cols, mine, *others, lower_inv, upper_inv,
        scratch=[pltpu.VMEM((NB, NB), F32)],
    )
    message, panel, old = call(
        functools.partial(rows_kernel, True), [shape(ROWS), shape(ROWS), shape(2 * CAP_SO)],
        place, pivots, ranks, work, old[0], *near, w, v, upper,
    )
    return finish(True, place, (pivots, ranks, matrix), old, top, panel, message)


def general(place, matrix, work, pivots, lower_inv, upper_inv, ranks, cols):
    row = place[0]
    pivots = pivots[0]
    here = (pivots >> 8) == row
    local = pivots & 255
    index = jnp.arange(NB, dtype=jnp.int32)
    top_here = (index >> 8) == row
    both = jnp.concatenate(
        [
            jnp.where(here[:, None], work[local], F32(0.0)),
            jnp.where(top_here[:, None], work[index & 255], F32(0.0)),
        ],
        axis=0,
    )
    for bit in (1, 2, 4, 8, 16, 32):
        both = both + lax.ppermute(both, "prow", [(i, i ^ bit) for i in range(XN * ZN)])
    top, old = both[:NB], both[NB:]
    swapped = work.at[jnp.where(here, local, ROWS)].set(old, mode="drop")
    w, v, upper = call(
        factor_kernel, [shape(NB), shape(NB), shape(ROWS)],
        place, top, lower_inv, upper_inv,
        scratch=[pltpu.VMEM((NB, NB), F32)],
    )
    message, panel = call(
        functools.partial(rows_kernel, False), [shape(ROWS)] * 2, place, swapped, w, v, upper
    )
    return finish(False, place, (), swapped, top, panel, message)


def per_device(matrix, pivots, lower_inv, upper_inv):
    place = jnp.stack([lax.axis_index("prow"), lax.axis_index("pcol")]).astype(jnp.int32)
    pivots = pivots.reshape(1, NB)
    work = swap_blocks(matrix)
    ranks, cols, fits = call(
        ranks_kernel,
        [shape(8, NB, jnp.int32), shape(NB, 8, jnp.int32), jax.ShapeDtypeStruct((1,), jnp.int32)],
        pivots,
        in_specs=[VMEM],
        out_specs=[VMEM, VMEM, SMEM],
    )
    return lax.cond(
        fits[0] == 1, direct, general,
        place, matrix, work, pivots, lower_inv, upper_inv, ranks, cols,
    )


def solution(mesh):
    in_specs = (P("prow", "pcol"), P(), P(), P())
    out_specs = P("prow", "pcol")
    return jax.shard_map(
        per_device, mesh=mesh, in_specs=in_specs, out_specs=out_specs, check_vma=False
    )
```
